32 devices in a mesh: grp: 2 (over y), sx: 4 (over x, core), sy: 4 (over z).
Axes of the slice: x: 2, y: 2, z: 4, core: 2. Of those that a mesh axis runs over, the one named last changes fastest.
Arguments:
- rhs_field: float32 [64, 64, 512], P(('grp', 'sx'), None, 'sy'), parts along dimension 0, may hold values from -6 to 6
- conduct: float32 [64, 64, 512], P(('grp', 'sx'), None, 'sy'), parts along dimension 0, may hold values from 0.05 to 5
- intersections: int32 [8, 2], P('grp'), parts along dimension 0, may hold values from 1 to 4, as said below
- poly_coef: float32 [4], replicated
Outputs:
- solution_field: float32 [64, 64, 512], P(('grp', 'sx'), None, 'sy'), parts along dimension 0
- residual: float32 [64, 64, 512], P(('grp', 'sx'), None, 'sy'), parts along dimension 0
The draws below stay inside these ranges and needn't reach their ends.
There are 2 independent parts, one for each index of `grp`. The reference program is written for one: setup_inputs(seed, part) draws one part's arguments, and reference() takes and returns one part's arrays. A program takes and returns all parts, laid end to end along the dimension named above; an argument that names none is the same for every part. Nothing has to cross between parts.
Inputs may be any that keep to these rules, and one draw needn't show every extreme that they name: `intersections`: 4 is reached in every draw.
All inputs are finite; a program needn't handle non-finite values.
Results may differ from the reference program's by a relative error of at most 0.0003.
Values sent between devices are 32-bit elements; how exact they have to be, the bound alone decides.
A program may use at most 128 MiB of HBM per device.

```python
import math
import jax
import jax.numpy as jnp

CX = 8
NZ = 64
OV = 4
DEG = 3
M = 4
NX = 32
NY = 512
NSUB = 4


def draw_intersections(key, part):
    key = jax.random.fold_in(key, 11)
    key_w, key_s, key_d = jax.random.split(key, 3)
    widths = jax.random.randint(key_w, (NSUB, 2), 1, OV + 1)
    spot = jax.random.randint(key_s, (), 0, NSUB)
    side = jax.random.randint(key_d, (), 0, 2)
    return widths.at[spot, side].set(OV).astype(jnp.int32)


def draw_poly_coef(key, part):
    key = jax.random.fold_in(key, 23)
    base = jnp.array([(-1) ** term * math.comb(DEG + 1, term + 1) for term in range(DEG + 1)], jnp.float32)
    factor = 1.0 + 0.08 * jnp.clip(jax.random.normal(key, (DEG + 1,), jnp.float32), -2.0, 2.0)
    return (base * factor).astype(jnp.float32)


def level_of(stream_key, shape, cuts, least, top_value):
    loudness = 1.0
    for dim, blocks in cuts:
        draws = jax.random.uniform(jax.random.fold_in(jax.random.fold_in(stream_key, 6), dim), (blocks,), jnp.float32, least / len(cuts), top_value / len(cuts))
        loudness = loudness * jnp.repeat(jnp.exp(draws), shape[dim] // blocks).reshape((-1,) + (1,) * (len(shape) - 1 - dim))
    return loudness


def noise(stream_key, dims, deviation, limit, cuts=(), kind=jnp.bfloat16):
    level = level_of(stream_key, dims, cuts, -0.22, 0.18) if cuts else 1.0
    values = jax.random.normal(stream_key, dims, jnp.float32) * deviation * level
    return jnp.minimum(jnp.maximum(values, -limit), limit).astype(kind)


def setup_inputs(seed: int = 0, part: int = 0) -> dict:
    arg_keys = jax.random.split(jax.random.key(seed), 5)
    part_splits = jax.random.split(jax.random.fold_in(arg_keys[4], part), 5)
    return {
        "rhs_field": noise(part_splits[0], (NX, NZ, NY), 1.0, 6.0, ((0, 4), (2, 4)), jnp.float32),
        "conduct": jnp.clip(jnp.exp(math.log(5.0) - 4.6051702 * jax.random.uniform(part_splits[1], (NX, NZ, NY), jnp.float32) ** level_of(part_splits[1], (NX, NZ, NY), ((0, 4), (2, 4)), -0.2, 0.2)), 0.05, 5.0),
        "intersections": draw_intersections(jax.random.fold_in(jax.random.fold_in(arg_keys[4], part), 71), part),
        "poly_coef": draw_poly_coef(jax.random.fold_in(arg_keys[4], 71), part),
    }


def five_point_operator(padded_vector, padded_krylov):
    center_krylov = padded_krylov[1:-1, :, 1:-1]
    center_vector = padded_vector[1:-1, :, 1:-1]
    grand_total = 0.5 * (center_krylov + padded_krylov[2:, :, 1:-1]) * (center_vector - padded_vector[2:, :, 1:-1])
    grand_total = grand_total + 0.5 * (center_krylov + padded_krylov[:-2, :, 1:-1]) * (center_vector - padded_vector[:-2, :, 1:-1])
    grand_total = grand_total + 0.5 * (center_krylov + padded_krylov[1:-1, :, 2:]) * (center_vector - padded_vector[1:-1, :, 2:])
    grand_total = grand_total + 0.5 * (center_krylov + padded_krylov[1:-1, :, :-2]) * (center_vector - padded_vector[1:-1, :, :-2])
    kvert = jnp.pad(center_krylov, ((0, 0), (1, 1), (0, 0)))
    vvert = jnp.pad(center_vector, ((0, 0), (1, 1), (0, 0)))
    grand_total = grand_total + 0.5 * (center_krylov + kvert[:, 2:]) * (center_vector - vvert[:, 2:])
    grand_total = grand_total + 0.5 * (center_krylov + kvert[:, :-2]) * (center_vector - vvert[:, :-2])
    return grand_total

def diagonal(padded_krylov):
    center_krylov = padded_krylov[1:-1, :, 1:-1]
    kvert = jnp.pad(center_krylov, ((0, 0), (1, 1), (0, 0)))
    grand_total = 0.5 * (center_krylov + padded_krylov[2:, :, 1:-1]) + 0.5 * (center_krylov + padded_krylov[:-2, :, 1:-1])
    grand_total = grand_total + 0.5 * (center_krylov + padded_krylov[1:-1, :, 2:]) + 0.5 * (center_krylov + padded_krylov[1:-1, :, :-2])
    grand_total = grand_total + 0.5 * (center_krylov + kvert[:, 2:]) + 0.5 * (center_krylov + kvert[:, :-2])
    return jnp.where(center_krylov > 0, grand_total, 1.0)

def operator(field, conduct):
    widths = ((1, 1), (0, 0), (1, 1))
    return five_point_operator(jnp.pad(field, widths), jnp.pad(conduct, widths))

def precondition(resid, conduct, intersections, poly_coef):
    extent = CX + 2 * OV
    resid_pad = jnp.pad(resid, ((OV, OV), (0, 0), (0, 0)))
    cond_pad = jnp.pad(conduct, ((OV + 1, OV + 1), (0, 0), (1, 1)))
    plane = jnp.arange(extent, dtype=jnp.int32)
    pieces = []
    for sub in range(NSUB):
        left = intersections[sub, 0]
        right = intersections[sub, 1]
        gpos = sub * CX + plane - OV
        keep = (plane >= OV - left) & (plane < OV + CX + right) & (gpos >= 0) & (gpos < NX)
        keep = keep[:, None, None]
        kslab = cond_pad[sub * CX:sub * CX + extent + 2]
        dslab = diagonal(kslab)
        level = jnp.where(keep, resid_pad[sub * CX:sub * CX + extent] / dslab, 0.0)
        result = poly_coef[0] * level[OV:OV + CX]
        for power in range(1, DEG + 1):
            padded = jnp.pad(level, ((1, 1), (0, 0), (1, 1)))
            level = jnp.where(keep, five_point_operator(padded, kslab) / dslab, 0.0)
            result = result + poly_coef[power] * level[OV:OV + CX]
        pieces.append(result)
    return jnp.concatenate(pieces, axis=0)

def least_squares(hmat, beta):
    rows = hmat
    target = jnp.zeros((M + 1,), jnp.float32).at[0].set(beta)
    for step in range(M):
        first = rows[step, step]
        second = rows[step + 1, step]
        radius = jnp.sqrt(first * first + second * second)
        cosine = first / radius
        sine_val = second / radius
        upper = cosine * rows[step] + sine_val * rows[step + 1]
        lower = -sine_val * rows[step] + cosine * rows[step + 1]
        rows = rows.at[step].set(upper).at[step + 1].set(lower)
        tgt_up = cosine * target[step] + sine_val * target[step + 1]
        tgt_low = -sine_val * target[step] + cosine * target[step + 1]
        target = target.at[step].set(tgt_up).at[step + 1].set(tgt_low)
    coeffs = [None] * M
    for step in reversed(range(M)):
        running = target[step]
        for later in range(step + 1, M):
            running = running - rows[step, later] * coeffs[later]
        coeffs[step] = running / rows[step, step]
    return coeffs

def reference(rhs_field, conduct, intersections, poly_coef):
    beta = jnp.sqrt(jnp.sum(rhs_field * rhs_field))
    basis = [rhs_field / beta]
    columns = []
    for step in range(M):
        image = operator(precondition(basis[step], conduct, intersections, poly_coef), conduct)
        proj = [jnp.sum(image * vec) for vec in basis]
        for which in range(step + 1):
            image = image - proj[which] * basis[which]
        new_len = jnp.sqrt(jnp.sum(image * image))
        basis.append(image / new_len)
        column = proj + [new_len] + [jnp.zeros((), jnp.float32)] * (M - step - 1)
        columns.append(jnp.stack(column))
    hmat = jnp.stack(columns, axis=1)
    coeffs = least_squares(hmat, beta)
    combined = coeffs[0] * basis[0]
    for step in range(1, M):
        combined = combined + coeffs[step] * basis[step]
    solution_field = precondition(combined, conduct, intersections, poly_coef)
    residual = rhs_field - operator(solution_field, conduct)
    return (solution_field, residual)
```

```python
import functools

import jax
import jax.numpy as jnp
from jax import lax
from jax.experimental import pallas as pl
from jax.experimental.pallas import tpu as pltpu
from jax.sharding import PartitionSpec as P

OV = 4
DEG = 3
M = 4
B = 8
MESH = pl.DeviceIdType.MESH
F32 = jnp.float32


def swap(a):
    return pltpu.roll(a, 64, a.ndim - 1)


def half_turn(a):
    return pltpu.roll(a, 4, a.ndim - 2)


def kernel(
    nsx, nsy, rhs_ref, cond_ref, inter_ref, coef_ref, sol_ref, res_ref,
    rc, kc, vb, qb, zb, sc, zc,
    fxp, fxm, fyp, fym, fzp, fzm, dg, inv, kx,
    ua, na, ub, nb, uc, nc, zx,
    pack, recx, recy, kxr, kyr, red1, red2,
    sem_sx, sem_rx, sem_sy, sem_ry, sem_ksx, sem_krx, sem_ksy, sem_kry,
    sem_s1, sem_r1, sem_s2, sem_r2,
):
    ix = lax.axis_index("sx")
    iy = lax.axis_index("sy")
    sub3 = lax.broadcasted_iota(jnp.int32, (1, 8, 128), 1)
    lane3 = lax.broadcasted_iota(jnp.int32, (1, 8, 128), 2)
    sub2 = lax.broadcasted_iota(jnp.int32, (8, 128), 0)
    own = lane3 < 64
    low = sub3 < 4
    depth = lane3 % 64

    def full(mask, size):
        return jnp.broadcast_to(mask, (size, 8, 128))

    recx[...] = jnp.zeros_like(recx)
    recy[...] = jnp.zeros_like(recy)
    kxr[...] = jnp.zeros_like(kxr)
    kyr[...] = jnp.zeros_like(kyr)

    def exists(dx, dy):
        return (ix + dx >= 0) & (ix + dx < nsx) & (iy + dy >= 0) & (iy + dy < nsy)

    def device(dx, dy):
        return {"sx": ix + dx, "sy": iy + dy}

    barrier = pltpu.get_barrier_semaphore()
    for d in range(1, nsx):
        pl.semaphore_signal(barrier, inc=1, device_id={"sx": lax.rem(ix + d, nsx), "sy": iy}, device_id_type=MESH)
    for d in range(1, nsy):
        pl.semaphore_signal(barrier, inc=1, device_id={"sx": ix, "sy": lax.rem(iy + d, nsy)}, device_id_type=MESH)
    corners = [(dx, dy) for dx in (-1, 1) for dy in (-1, 1)]
    for dx, dy in corners:
        @pl.when(exists(dx, dy))
        def _():
            pl.semaphore_signal(barrier, inc=1, device_id=device(dx, dy), device_id_type=MESH)

    def load_packed(src, dst):
        planes = []
        for x in range(8):
            a = src[x]
            both = jnp.concatenate([a[:, :64], a[:, 64:]], axis=0)
            planes.append(both.T)
        dst[...] = jnp.swapaxes(jnp.stack(planes, axis=0), 0, 1)

    load_packed(cond_ref, kc)
    load_packed(rhs_ref, rc)
    for ref in (ua, na, ub, nb, uc, nc, zx):
        ref[0:1] = jnp.zeros((1, 8, 128), F32)
        ref[137:138] = jnp.zeros((1, 8, 128), F32)

    peers = nsx - 1 + nsy - 1
    for dx, dy in corners:
        peers = peers + exists(dx, dy).astype(jnp.int32)
    pl.semaphore_wait(barrier, peers)

    def x_copies(make):
        return [(exists(side, 0), exists(-side, 0), make(side, slot)) for slot, side in enumerate((-1, 1))]

    def y_copies(make):
        out = []
        for slot, (dx, dy) in enumerate([(dx, dy) for dy in (-1, 1) for dx in (-1, 0, 1)]):
            out.append((exists(dx, dy), exists(-dx, -dy), make(dx, dy, slot)))
        return out

    def k_copies():
        def make_x(side, slot):
            return pltpu.make_async_remote_copy(
                kc, kxr.at[slot], sem_ksx.at[slot], sem_krx.at[slot],
                device_id=device(side, 0), device_id_type=MESH)

        def make_y(dx, dy, slot):
            src = kc.at[pl.ds(0, OV + 1)] if dy < 0 else kc.at[pl.ds(64 - OV - 1, OV + 1)]
            return pltpu.make_async_remote_copy(
                src, kyr.at[slot], sem_ksy.at[slot], sem_kry.at[slot],
                device_id=device(dx, dy), device_id_type=MESH)

        return x_copies(make_x) + y_copies(make_y)

    def f_copies(phase, field):
        def make_x(side, slot):
            return pltpu.make_async_remote_copy(
                pack.at[phase, slot], recx.at[phase, slot], sem_sx.at[phase, slot], sem_rx.at[phase, slot],
                device_id=device(side, 0), device_id_type=MESH)

        def make_y(dx, dy, slot):
            src = field.at[pl.ds(0, OV)] if dy < 0 else field.at[pl.ds(64 - OV, OV)]
            return pltpu.make_async_remote_copy(
                src, recy.at[phase, slot], sem_sy.at[phase, slot], sem_ry.at[phase, slot],
                device_id=device(dx, dy), device_id_type=MESH)

        return x_copies(make_x) + y_copies(make_y)

    def start(copies):
        for sends, _, copy in copies:
            pl.when(sends)(copy.start)

    def arrive(copies):
        for _, receives, copy in copies:
            pl.when(receives)(copy.wait_recv)

    def leave(copies):
        for sends, _, copy in copies:
            pl.when(sends)(copy.wait_send)

    def red_copies(phase, stage, sending):
        buf, ssem, rsem, n, me = (
            (red1, sem_s1, sem_r1, nsx, ix) if stage == 0 else (red2, sem_s2, sem_r2, nsy, iy))
        out = []
        for d in range(1, n):
            other = lax.rem(me + d, n)
            where = {"sx": other, "sy": iy} if stage == 0 else {"sx": ix, "sy": other}
            slot = me if sending else other
            out.append(pltpu.make_async_remote_copy(
                buf.at[phase, slot], buf.at[phase, slot], ssem.at[phase, d], rsem.at[phase, slot],
                device_id=where, device_id_type=MESH))
        return out

    def red_start(phase, stage, tile):
        if stage == 0:
            red1[phase, ix] = tile
        else:
            red2[phase, iy] = tile
        for copy in red_copies(phase, stage, True):
            copy.start()

    def red_finish(phase, stage):
        for copy in red_copies(phase, stage, False):
            copy.wait_recv()
        buf, n = (red1, nsx) if stage == 0 else (red2, nsy)
        total = buf[phase, 0]
        for i in range(1, n):
            total = total + buf[phase, i]
        return total

    def tile_of(accs):
        tile = jnp.zeros((8, 128), F32)
        for i, acc in enumerate(accs):
            tile = jnp.where(sub2 == i, jnp.broadcast_to(jnp.sum(acc, axis=0, keepdims=True), (8, 128)), tile)
        return tile

    def rows_of(total, n):
        sums = jnp.broadcast_to(jnp.sum(total, axis=1, keepdims=True), (8, 128))
        return [jnp.broadcast_to(sums[i:i + 1], (8, 128)) for i in range(n)]

    def pack_pair(phase, i, lo, hi):
        size = lo.shape[0]
        pack[phase, 0, pl.ds(i, size)] = jnp.where(full(low, size), lo, half_turn(hi))
        pack[phase, 1, pl.ds(i, size)] = jnp.where(full(low, size), half_turn(lo), hi)

    def loop(n, body, carry=None):
        return lax.fori_loop(0, n, body, carry)

    def ring_pair(c, r):
        size = c.shape[0]
        o = full(own, size)
        mixed = swap(jnp.where(o, r, c))
        return jnp.where(o, c, mixed), jnp.where(o, mixed, r)

    def ring_sides(buf, size):
        o, lo = full(own, size), full(low, size)
        above = jnp.where(o, buf[1], swap(jnp.where(lo, buf[0], buf[2])))
        below = jnp.where(o, swap(buf[4]), jnp.where(lo, buf[3], buf[5]))
        return above, below

    kcop = k_copies()
    start(kcop)

    def first(i, acc):
        lo = rc[pl.ds(i * B, B)]
        hi = rc[pl.ds(i * B + 32, B)]
        pack_pair(0, i * B, lo, hi)
        return acc + jnp.sum(lo * lo + hi * hi, axis=0)

    acc = loop(32 // B, first, jnp.zeros((8, 128), F32))
    copies = [f_copies(0, rc)]
    start(copies[0])
    red_start(0, 0, tile_of([acc]))

    arrive(kcop)

    def k_ring(i, _):
        c = kc[pl.ds(i * B, B)]
        r = jnp.where(full(low, B), kxr[0, pl.ds(i * B, B)], kxr[1, pl.ds(i * B, B)])
        a, b = ring_pair(c, r)
        kx[pl.ds(i * B + 5, B)] = a
        kx[pl.ds(i * B + 69, B)] = b
        return None

    loop(64 // B, k_ring)
    above, below = ring_sides(kyr, OV + 1)
    kx[133:138] = above
    kx[0:5] = below

    def far(i, slot):
        return kxr[slot, pl.ds(i, B)]

    def x_plus(a, size):
        return pltpu.roll(jnp.where(full(sub3 == 0, size), swap(a), a), 7, 1)

    def x_minus(a, size):
        return pltpu.roll(jnp.where(full(sub3 == 7, size), swap(a), a), 1, 1)

    end_plus = (lane3 >= 64) & (sub3 == 3)
    end_minus = (lane3 >= 64) & (sub3 == 4)
    top = depth == 63
    bottom = depth == 0

    def coefficients(at, size, beyond_plus, beyond_minus):
        k = kx[pl.ds(at, size)]
        kxp = jnp.where(full(end_plus, size), beyond_plus, x_plus(k, size))
        kxm = jnp.where(full(end_minus, size), beyond_minus, x_minus(k, size))
        kzp = jnp.where(full(top, size), 0.0, pltpu.roll(k, 127, 2))
        kzm = jnp.where(full(bottom, size), 0.0, pltpu.roll(k, 1, 2))
        xp = 0.5 * (k + kxp)
        xm = 0.5 * (k + kxm)
        yp = 0.5 * (k + kx[pl.ds(at + 1, size)])
        ym = 0.5 * (k + kx[pl.ds(at - 1, size)])
        zp = 0.5 * (k + kzp)
        zm = 0.5 * (k + kzm)
        diag = xp + xm + yp + ym + zp + zm
        inside = k > 0
        recip = jnp.where(inside, 1.0 / jnp.where(inside, diag, 1.0), 0.0)
        put = pl.ds(at, size)
        fxp[put] = xp * recip
        fxm[put] = xm * recip
        fyp[put] = yp * recip
        fym[put] = ym * recip
        fzp[put] = jnp.where(full(top, size), 0.0, zp * recip)
        fzm[put] = jnp.where(full(bottom, size), 0.0, zm * recip)
        inv[put] = recip
        dg[put] = jnp.where(full(own, size), diag, 0.0)

    def coef_body(i, _):
        p = pltpu.roll(kxr[0, pl.ds(i * B, B)], 7, 1)
        m = pltpu.roll(kxr[1, pl.ds(i * B, B)], 1, 1)
        coefficients(i * B + 5, B, swap(p), swap(m))
        coefficients(i * B + 69, B, p, m)
        return None

    loop(64 // B, coef_body)
    coefficients(133, 4, swap(pltpu.roll(kyr[0, 0:4], 7, 1)), swap(pltpu.roll(kyr[2, 0:4], 1, 1)))
    coefficients(1, 4, pltpu.roll(kyr[3, 1:5], 7, 1), pltpu.roll(kyr[5, 1:5], 1, 1))

    before = jnp.maximum(ix - 1, 0)
    after = jnp.minimum(ix + 1, nsx - 1)
    left, right = inter_ref[ix, 0], inter_ref[ix, 1]
    right_before, left_after = inter_ref[before, 1], inter_ref[after, 0]
    keep = own | (low & (sub3 < right)) | ((sub3 >= 4) & (sub3 >= 8 - left))
    keep_near = (lane3 >= 64) | (low & (sub3 < right_before)) | ((sub3 >= 4) & (sub3 >= 8 - left_after))
    keep = jnp.where(keep, 1.0, 0.0).astype(F32)
    keep_near = jnp.where(keep_near, 1.0, 0.0).astype(F32)

    def neighbours(at, size, srcs):
        put = pl.ds(at, size)
        cs = [f[put] for f in (fxp, fxm, fyp, fym, fzp, fzm)]
        outs = []
        for src in srcs:
            a = src[put]
            sw = swap(a)
            xp = pltpu.roll(jnp.where(full(sub3 == 0, size), sw, a), 7, 1)
            xm = pltpu.roll(jnp.where(full(sub3 == 7, size), sw, a), 1, 1)
            s = cs[0] * xp + cs[1] * xm
            s = s + (cs[2] * src[pl.ds(at + 1, size)] + cs[3] * src[pl.ds(at - 1, size)])
            s = s + (cs[4] * pltpu.roll(a, 127, 2) + cs[5] * pltpu.roll(a, 1, 2))
            outs.append(a - s)
        return outs

    def precondition_image(phase):
        def begin(at, field):
            put = pl.ds(at, field.shape[0])
            u = field * inv[put]
            ua[put] = u * keep
            na[put] = u * keep_near

        field = rc if phase == 0 else qb.at[phase - 1]

        def enter(i, _):
            a, b = recx[phase, 0, pl.ds(i * B, B)], recx[phase, 1, pl.ds(i * B, B)]
            r_lo = jnp.where(full(low, B), a, half_turn(b))
            r_hi = jnp.where(full(low, B), half_turn(a), b)
            for base, r in ((0, r_lo), (32, r_hi)):
                f, g = ring_pair(field[pl.ds(i * B + base, B)], r)
                begin(i * B + base + 5, f)
                begin(i * B + base + 69, g)
            return None

        loop(32 // B, enter)
        above, below = ring_sides(recy.at[phase], OV)
        begin(133, above)
        begin(1, below)

        for src, dst in (((ua, na), (ub, nb)), ((ub, nb), (uc, nc))):
            def power(i, _):
                at = i * B + 1
                u, n = neighbours(at, B, src)
                dst[0][pl.ds(at, B)] = u * keep
                dst[1][pl.ds(at, B)] = n * keep_near
                return None

            loop(136 // B, power)

        def last(i, _):
            at = i * B + 1
            put = pl.ds(at, B)
            u, n = neighbours(at, B, (uc, nc))
            o = full(own, B)
            u3 = jnp.where(o, u, n)
            u2 = jnp.where(o, uc[put], nc[put])
            u1 = jnp.where(o, ub[put], nb[put])
            u0 = jnp.where(o, ua[put], na[put])
            zx[put] = coef_ref[0] * u0 + coef_ref[1] * u1 + coef_ref[2] * u2 + coef_ref[3] * u3
            return None

        loop(136 // B, last)

        def image(i, _):
            at = i * B + 5
            o = full(own, B)
            lo = neighbours(at, B, (zx,))[0] * dg[pl.ds(at, B)]
            hi = neighbours(at + 64, B, (zx,))[0] * dg[pl.ds(at + 64, B)]
            sc[pl.ds(i * B, B)] = jnp.where(o, lo, swap(hi))
            zc[pl.ds(i * B, B)] = jnp.where(o, zx[pl.ds(at, B)], swap(zx[pl.ds(at + 64, B)]))
            return None

        loop(64 // B, image)

    hcols = []
    beta = None
    for k in range(M):
        arrive(copies[k])
        red_start(k, 1, red_finish(k, 0))
        precondition_image(k)
        rows = rows_of(red_finish(k, 1), k + 1)
        if k == 0:
            beta = jnp.sqrt(rows[0])
            scale = 1.0 / beta
            h = []
        else:
            h = rows[:k]
            square = rows[k]
            for x in h:
                square = square - x * x
            length = jnp.sqrt(square)
            scale = 1.0 / length
            hcols.append(h + [length])

        def update(i, accs, k=k, h=h, scale=scale):
            accs = list(accs)
            fields = []
            for base in (0, 32):
                put = pl.ds(i * B + base, B)
                v = rc[put] if k == 0 else qb[k - 1, put]
                q = sc[put]
                z = zc[put]
                basis = [vb[j, put] for j in range(k)]
                for j in range(k):
                    v = v - h[j] * basis[j]
                    q = q - h[j] * qb[j, put]
                    z = z - h[j] * zb[j, put]
                v, q, z = v * scale, q * scale, z * scale
                vb[k, put] = v
                qb[k, put] = q
                zb[k, put] = z
                for j, b in enumerate(basis + [v, q]):
                    accs[j] = accs[j] + jnp.sum(q * b, axis=0)
                fields.append(q)
            if k < M - 1:
                pack_pair(k + 1, i * B, fields[0], fields[1])
            return tuple(accs)

        accs = loop(32 // B, update, tuple(jnp.zeros((8, 128), F32) for _ in range(k + 2)))
        if k < M - 1:
            copies.append(f_copies(k + 1, qb.at[k]))
            start(copies[k + 1])
        red_start(k + 1, 0, tile_of(accs))

    red_start(M, 1, red_finish(M, 0))
    rows = rows_of(red_finish(M, 1), M + 1)
    square = rows[M]
    for x in rows[:M]:
        square = square - x * x
    hcols.append(rows[:M] + [jnp.sqrt(square)])

    g = [beta] + [jnp.zeros((8, 128), F32)] * M
    turns = []
    upper = []
    for k in range(M):
        col = list(hcols[k])
        for j, (c, s) in enumerate(turns):
            col[j], col[j + 1] = c * col[j] + s * col[j + 1], c * col[j + 1] - s * col[j]
        rad = jnp.sqrt(col[k] * col[k] + col[k + 1] * col[k + 1])
        c, s = col[k] / rad, col[k + 1] / rad
        turns.append((c, s))
        col[k] = c * col[k] + s * col[k + 1]
        upper.append(col)
        g[k], g[k + 1] = c * g[k] + s * g[k + 1], c * g[k + 1] - s * g[k]
    y = [None] * M
    for k in reversed(range(M)):
        run = g[k]
        for later in range(k + 1, M):
            run = run - upper[later][k] * y[later]
        y[k] = run / upper[k][k]

    def combine(i, _):
        put = pl.ds(i * B, B)
        z = y[0] * zb[0, put]
        r = rc[put] - y[0] * qb[0, put]
        for k in range(1, M):
            z = z + y[k] * zb[k, put]
            r = r - y[k] * qb[k, put]
        zc[put] = z
        sc[put] = r
        return None

    loop(64 // B, combine)

    def store_packed(src, dst):
        planes = jnp.swapaxes(src[...], 0, 1)
        for x in range(8):
            t = planes[x].T
            dst[x] = jnp.concatenate([t[:64], t[64:]], axis=1)

    store_packed(zc, sol_ref)
    store_packed(sc, res_ref)

    leave(kcop)
    for c in copies:
        leave(c)
    for phase in range(M + 1):
        for stage in range(2):
            for copy in red_copies(phase, stage, True):
                copy.wait_send()


def local(nsx, nsy, rhs_field, conduct, intersections, poly_coef):
    assert rhs_field.shape == (8, 64, 128)
    vmem = pl.BlockSpec(memory_space=pltpu.VMEM)
    smem = pl.BlockSpec(memory_space=pltpu.SMEM)
    packed = (64, 8, 128)
    ring = (138, 8, 128)
    dma = pltpu.SemaphoreType.DMA
    scratch = (
        [pltpu.VMEM(packed, F32)] * 2
        + [pltpu.VMEM((M,) + packed, F32)] * 3
        + [pltpu.VMEM(packed, F32)] * 2
        + [pltpu.VMEM(ring, F32)] * 16
        + [
            pltpu.VMEM((M, 2, 32, 8, 128), F32),
            pltpu.VMEM((M, 2, 32, 8, 128), F32),
            pltpu.VMEM((M, 6, OV, 8, 128), F32),
            pltpu.VMEM((2,) + packed, F32),
            pltpu.VMEM((6, OV + 1, 8, 128), F32),
            pltpu.VMEM((M + 1, nsx, 8, 128), F32),
            pltpu.VMEM((M + 1, nsy, 8, 128), F32),
            dma((M, 2)), dma((M, 2)), dma((M, 6)), dma((M, 6)),
            dma((2,)), dma((2,)), dma((6,)), dma((6,)),
            dma((M + 1, nsx)), dma((M + 1, nsx)), dma((M + 1, nsy)), dma((M + 1, nsy)),
        ]
    )
    out = jax.ShapeDtypeStruct(rhs_field.shape, F32)
    return pl.pallas_call(
        functools.partial(kernel, nsx, nsy),
        out_shape=(out, out),
        in_specs=[vmem, vmem, smem, smem],
        out_specs=(vmem, vmem),
        scratch_shapes=scratch,
        compiler_params=pltpu.CompilerParams(
            collective_id=0, has_side_effects=True, vmem_limit_bytes=40 * 1024 * 1024
        ),
        name="gmres_cycle",
    )(rhs_field, conduct, intersections, poly_coef)


def solution(mesh):
    nsx, nsy = mesh.shape["sx"], mesh.shape["sy"]
    spec = P(("grp", "sx"), None, "sy")
    return jax.shard_map(
        functools.partial(local, nsx, nsy),
        mesh=mesh,
        in_specs=(spec, spec, P("grp", None), P()),
        out_specs=(spec, spec),
        check_vma=False,
    )
```

```python
import functools

import jax
import jax.numpy as jnp
from jax import lax
from jax.experimental import pallas as pl
from jax.experimental.pallas import tpu as pltpu
from jax.sharding import PartitionSpec as P

OV = 4
DEG = 3
M = 4
B = 32
PB = 34
MESH = pl.DeviceIdType.MESH
F32 = jnp.float32


def swap(a):
    return pltpu.roll(a, 64, a.ndim - 1)


def half_turn(a):
    return pltpu.roll(a, 4, a.ndim - 2)


def kernel(
    nsx, nsy, rhs_ref, cond_ref, inter_ref, coef_ref, sol_ref, res_ref,
    rc, kc, vb, qb, zb, sc, zc,
    fxp, fxm, fyp, fym, fzp, fzm, dg, inv, kx,
    ua, na, ub, nb, uc, nc, zx,
    pack, ypack, recx, recy, kxr, kyr, red1, red2,
    sem_sx, sem_rx, sem_sy, sem_ry, sem_ksx, sem_krx, sem_ksy, sem_kry,
    sem_s1, sem_r1, sem_s2, sem_r2,
):
    ix = lax.axis_index("sx")
    iy = lax.axis_index("sy")
    sub3 = lax.broadcasted_iota(jnp.int32, (1, 8, 128), 1)
    lane3 = lax.broadcasted_iota(jnp.int32, (1, 8, 128), 2)
    sub2 = lax.broadcasted_iota(jnp.int32, (8, 128), 0)

    def own(s, l):
        return l < 64

    def low(s, l):
        return s < 4

    def middle(s, l):
        return (s == 3) | (s == 4)

    def first_sub(s, l):
        return s == 0

    def last_sub(s, l):
        return s == 7

    def full(mask, size):
        shape = (size, 8, 128)
        return mask(lax.broadcasted_iota(jnp.int32, shape, 1), lax.broadcasted_iota(jnp.int32, shape, 2))

    recx[...] = jnp.zeros_like(recx)
    recy[...] = jnp.zeros_like(recy)
    kxr[...] = jnp.zeros_like(kxr)
    kyr[...] = jnp.zeros_like(kyr)

    def exists(dx, dy):
        return (ix + dx >= 0) & (ix + dx < nsx) & (iy + dy >= 0) & (iy + dy < nsy)

    def device(dx, dy):
        return {"sx": ix + dx, "sy": iy + dy}

    direct = nsx * nsy <= 16
    slots = nsx * nsy if direct else nsx
    others = [(dx, dy) for dx in range(nsx) for dy in range(nsy) if (dx, dy) != (0, 0)]

    def around(dx, dy):
        return {"sx": lax.rem(ix + dx, nsx), "sy": lax.rem(iy + dy, nsy)}

    barrier = pltpu.get_barrier_semaphore()
    if direct:
        for dx, dy in others:
            pl.semaphore_signal(barrier, inc=1, device_id=around(dx, dy), device_id_type=MESH)
    for d in range(1, nsx if not direct else 0):
        pl.semaphore_signal(barrier, inc=1, device_id={"sx": lax.rem(ix + d, nsx), "sy": iy}, device_id_type=MESH)
    for d in range(1, nsy if not direct else 0):
        pl.semaphore_signal(barrier, inc=1, device_id={"sx": ix, "sy": lax.rem(iy + d, nsy)}, device_id_type=MESH)
    corners = [] if direct else [(dx, dy) for dx in (-1, 1) for dy in (-1, 1)]
    for dx, dy in corners:
        @pl.when(exists(dx, dy))
        def _():
            pl.semaphore_signal(barrier, inc=1, device_id=device(dx, dy), device_id_type=MESH)

    def load_packed(src, dst):
        planes = []
        for x in range(8):
            a = src[x]
            both = jnp.concatenate([a[:, :64], a[:, 64:]], axis=0)
            planes.append(both.T)
        dst[...] = jnp.swapaxes(jnp.stack(planes, axis=0), 0, 1)

    load_packed(cond_ref, kc)
    load_packed(rhs_ref, rc)
    for ref in (ua, na, ub, nb, uc, nc, zx):
        ref[0:1] = jnp.zeros((1, 8, 128), F32)
        ref[137:138] = jnp.zeros((1, 8, 128), F32)

    peers = len(others) if direct else nsx - 1 + nsy - 1
    for dx, dy in corners:
        peers = peers + exists(dx, dy).astype(jnp.int32)
    pl.semaphore_wait(barrier, peers)

    def x_copies(make):
        return [(exists(side, 0), exists(-side, 0), make(side, slot)) for slot, side in enumerate((-1, 1))]

    def y_copies(make):
        out = []
        for slot, (dx, dy) in enumerate([(dx, dy) for dy in (-1, 1) for dx in (-1, 0, 1)]):
            out.append((exists(dx, dy), exists(-dx, -dy), make(dx, dy, slot)))
        return out

    def k_copies():
        def make_x(side, slot):
            return pltpu.make_async_remote_copy(
                kc, kxr.at[slot], sem_ksx.at[slot], sem_krx.at[slot],
                device_id=device(side, 0), device_id_type=MESH)

        def make_y(dx, dy, slot):
            src = kc.at[pl.ds(0, OV + 1)] if dy < 0 else kc.at[pl.ds(64 - OV - 1, OV + 1)]
            return pltpu.make_async_remote_copy(
                src, kyr.at[slot], sem_ksy.at[slot], sem_kry.at[slot],
                device_id=device(dx, dy), device_id_type=MESH)

        return x_copies(make_x) + y_copies(make_y)

    def f_copies(phase):
        def make_x(side, slot):
            return pltpu.make_async_remote_copy(
                pack.at[phase, slot], recx.at[phase, slot], sem_sx.at[phase, slot], sem_rx.at[phase, slot],
                device_id=device(side, 0), device_id_type=MESH)

        def make_y(dx, dy, slot):
            strip = ypack.at[phase, 0 if dy < 0 else 1]
            src = {0: strip.at[pl.ds(0, 2)], -1: strip.at[pl.ds(2, 1)], 1: strip.at[pl.ds(3, 1)]}[dx]
            dst = recy.at[phase, slot] if dx == 0 else recy.at[phase, slot, pl.ds(0, 1)]
            return pltpu.make_async_remote_copy(
                src, dst, sem_sy.at[phase, slot], sem_ry.at[phase, slot],
                device_id=device(dx, dy), device_id_type=MESH)

        return x_copies(make_x) + y_copies(make_y)

    def start(copies):
        for sends, _, copy in copies:
            pl.when(sends)(copy.start)

    def arrive(copies):
        for _, receives, copy in copies:
            pl.when(receives)(copy.wait_recv)

    def leave(copies):
        for sends, _, copy in copies:
            pl.when(sends)(copy.wait_send)

    def red_copies(phase, stage, sending):
        if direct:
            out = []
            for dx, dy in others:
                where = around(dx, dy)
                slot = ix * nsy + iy if sending else where["sx"] * nsy + where["sy"]
                out.append(pltpu.make_async_remote_copy(
                    red1.at[phase, slot], red1.at[phase, slot], sem_s1.at[phase, dx * nsy + dy], sem_r1.at[phase, slot],
                    device_id=where, device_id_type=MESH))
            return out
        buf, ssem, rsem, n, me = (
            (red1, sem_s1, sem_r1, nsx, ix) if stage == 0 else (red2, sem_s2, sem_r2, nsy, iy))
        out = []
        for d in range(1, n):
            other = lax.rem(me + d, n)
            where = {"sx": other, "sy": iy} if stage == 0 else {"sx": ix, "sy": other}
            slot = me if sending else other
            out.append(pltpu.make_async_remote_copy(
                buf.at[phase, slot], buf.at[phase, slot], ssem.at[phase, d], rsem.at[phase, slot],
                device_id=where, device_id_type=MESH))
        return out

    def red_start(phase, stage, tile):
        if stage == 0:
            red1[phase, ix * nsy + iy if direct else ix] = tile
        else:
            red2[phase, iy] = tile
        for copy in red_copies(phase, stage, True):
            copy.start()

    def red_finish(phase, stage):
        for copy in red_copies(phase, stage, False):
            copy.wait_recv()
        buf, n = (red1, slots) if stage == 0 else (red2, nsy)
        terms = [buf[phase, i] for i in range(n)]
        while len(terms) > 1:
            terms = [sum(terms[i:i + 2][1:], terms[i]) for i in range(0, len(terms), 2)]
        return terms[0]

    def red_middle(phase):
        if not direct:
            red_start(phase, 1, red_finish(phase, 0))

    def red_end(phase):
        return red_finish(phase, 0 if direct else 1)

    def tile_of(accs):
        tile = jnp.zeros((8, 128), F32)
        for i, acc in enumerate(accs):
            tile = jnp.where(sub2 == i, jnp.broadcast_to(jnp.sum(acc, axis=0, keepdims=True), (8, 128)), tile)
        return tile

    def rows_of(total, n):
        sums = jnp.broadcast_to(jnp.sum(total, axis=1, keepdims=True), (8, 128))
        return [jnp.broadcast_to(sums[i:i + 1], (8, 128)) for i in range(n)]

    def pack_pair(phase, i, lo, hi):
        size = lo.shape[0]
        pack[phase, 0, pl.ds(i, size)] = jnp.where(full(low, size), lo, half_turn(hi))
        pack[phase, 1, pl.ds(i, size)] = jnp.where(full(low, size), half_turn(lo), hi)

    def pack_strips(phase, field):
        o = full(own, 2)
        c, d = field[0:4], field[60:64]
        for side, p in enumerate((jnp.where(o, c[0:2], swap(c[2:4])), jnp.where(o, swap(d[0:2]), d[2:4]))):
            ypack[phase, side, 0:2] = p
            lo = full(low, 1)
            ypack[phase, side, 2:3] = jnp.where(lo, p[0:1], half_turn(p[1:2]))
            ypack[phase, side, 3:4] = jnp.where(lo, half_turn(p[0:1]), p[1:2])

    def loop(n, body, carry=None):
        return lax.fori_loop(0, n, body, carry)

    def ring_pair(c, r):
        size = c.shape[0]
        o = full(own, size)
        mixed = swap(jnp.where(o, r, c))
        return jnp.where(o, c, mixed), jnp.where(o, mixed, r)

    def ring_sides(buf, size):
        o, lo = full(own, size), full(low, size)
        above = jnp.where(o, buf[1], swap(jnp.where(lo, buf[0], buf[2])))
        below = jnp.where(o, swap(buf[4]), jnp.where(lo, buf[3], buf[5]))
        return above, below

    kcop = k_copies()
    start(kcop)

    def first(i, acc):
        lo = rc[pl.ds(i * B, B)]
        hi = rc[pl.ds(i * B + 32, B)]
        pack_pair(0, i * B, lo, hi)
        return acc + jnp.sum(lo * lo + hi * hi, axis=0)

    acc = loop(32 // B, first, jnp.zeros((8, 128), F32))
    pack_strips(0, rc)
    copies = [f_copies(0)]
    start(copies[0])
    red_start(0, 0, tile_of([acc]))

    arrive(kcop)

    def k_ring(i, _):
        c = kc[pl.ds(i * B, B)]
        r = jnp.where(full(low, B), kxr[0, pl.ds(i * B, B)], kxr[1, pl.ds(i * B, B)])
        a, b = ring_pair(c, r)
        kx[pl.ds(i * B + 5, B)] = a
        kx[pl.ds(i * B + 69, B)] = b
        return None

    loop(64 // B, k_ring)
    above, below = ring_sides(kyr, OV + 1)
    kx[133:138] = above
    kx[0:5] = below

    def far(i, slot):
        return kxr[slot, pl.ds(i, B)]

    def x_plus(a, size):
        return pltpu.roll(jnp.where(full(first_sub, size), swap(a), a), 7, 1)

    def x_minus(a, size):
        return pltpu.roll(jnp.where(full(last_sub, size), swap(a), a), 1, 1)

    def end_plus(s, l):
        return (l >= 64) & (s == 3)

    def end_minus(s, l):
        return (l >= 64) & (s == 4)

    def top(s, l):
        return l % 64 == 63

    def bottom(s, l):
        return l % 64 == 0

    def coefficients(at, size, beyond_plus, beyond_minus):
        k = kx[pl.ds(at, size)]
        kxp = jnp.where(full(end_plus, size), beyond_plus, x_plus(k, size))
        kxm = jnp.where(full(end_minus, size), beyond_minus, x_minus(k, size))
        kzp = jnp.where(full(top, size), 0.0, pltpu.roll(k, 127, 2))
        kzm = jnp.where(full(bottom, size), 0.0, pltpu.roll(k, 1, 2))
        xp = 0.5 * (k + kxp)
        xm = 0.5 * (k + kxm)
        yp = 0.5 * (k + kx[pl.ds(at + 1, size)])
        ym = 0.5 * (k + kx[pl.ds(at - 1, size)])
        zp = 0.5 * (k + kzp)
        zm = 0.5 * (k + kzm)
        diag = xp + xm + yp + ym + zp + zm
        inside = k > 0
        recip = jnp.where(inside, 1.0 / jnp.where(inside, diag, 1.0), 0.0)
        put = pl.ds(at, size)
        fxp[put] = xp * recip
        fxm[put] = xm * recip
        fyp[put] = yp * recip
        fym[put] = ym * recip
        fzp[put] = jnp.where(full(top, size), 0.0, zp * recip)
        fzm[put] = jnp.where(full(bottom, size), 0.0, zm * recip)
        inv[put] = recip
        dg[put] = jnp.where(full(own, size), diag, 0.0)

    def coef_body(i, _):
        p = pltpu.roll(kxr[0, pl.ds(i * B, B)], 7, 1)
        m = pltpu.roll(kxr[1, pl.ds(i * B, B)], 1, 1)
        coefficients(i * B + 5, B, swap(p), swap(m))
        coefficients(i * B + 69, B, p, m)
        return None

    loop(64 // B, coef_body)
    coefficients(133, 4, swap(pltpu.roll(kyr[0, 0:4], 7, 1)), swap(pltpu.roll(kyr[2, 0:4], 1, 1)))
    coefficients(1, 4, pltpu.roll(kyr[3, 1:5], 7, 1), pltpu.roll(kyr[5, 1:5], 1, 1))

    before = jnp.maximum(ix - 1, 0)
    after = jnp.minimum(ix + 1, nsx - 1)
    left, right = inter_ref[ix, 0], inter_ref[ix, 1]
    right_before, left_after = inter_ref[before, 1], inter_ref[after, 0]
    keep = (lane3 < 64) | ((sub3 < 4) & (sub3 < right)) | ((sub3 >= 4) & (sub3 >= 8 - left))
    keep_near = (lane3 >= 64) | ((sub3 < 4) & (sub3 < right_before)) | ((sub3 >= 4) & (sub3 >= 8 - left_after))
    keep = jnp.where(keep, 1.0, 0.0).astype(F32)
    keep_near = jnp.where(keep_near, 1.0, 0.0).astype(F32)

    def neighbours(at, size, srcs):
        put = pl.ds(at, size)
        cs = [f[put] for f in (fxp, fxm, fyp, fym, fzp, fzm)]
        outs = []
        if len(srcs) == 2:
            both = swap(jnp.where(full(middle, size), half_turn(srcs[1][put]), srcs[0][put]))
            sws = (both, half_turn(both))
        for src in srcs:
            w = src[pl.ds(at - 1, size + 2)]
            a = w[1:size + 1]
            sw = swap(a) if len(srcs) == 1 else sws[src is srcs[1]]
            xp = pltpu.roll(jnp.where(full(first_sub, size), sw, a), 7, 1)
            xm = pltpu.roll(jnp.where(full(last_sub, size), sw, a), 1, 1)
            s = cs[0] * xp + cs[1] * xm
            s = s + (cs[2] * w[2:] + cs[3] * w[:size])
            s = s + (cs[4] * pltpu.roll(a, 127, 2) + cs[5] * pltpu.roll(a, 1, 2))
            outs.append(a - s)
        return outs

    def precondition_image(phase):
        def begin(at, field):
            put = pl.ds(at, field.shape[0])
            u = field * inv[put]
            ua[put] = u * keep
            na[put] = u * keep_near

        field = rc if phase == 0 else qb.at[phase - 1]

        def enter(i, _):
            a, b = recx[phase, 0, pl.ds(i * B, B)], recx[phase, 1, pl.ds(i * B, B)]
            r_lo = jnp.where(full(low, B), a, half_turn(b))
            r_hi = jnp.where(full(low, B), half_turn(a), b)
            for base, r in ((0, r_lo), (32, r_hi)):
                f, g = ring_pair(field[pl.ds(i * B + base, B)], r)
                begin(i * B + base + 5, f)
                begin(i * B + base + 69, g)
            return None

        loop(32 // B, enter)
        lo = full(low, 1)
        for slot, at in ((0, 133), (3, 1)):
            p = recy[phase, slot + 1]
            a, b = recy[phase, slot, 0:1], recy[phase, slot + 2, 0:1]
            r = jnp.concatenate([jnp.where(lo, a, half_turn(b)), jnp.where(lo, half_turn(a), b)], axis=0)
            f, g = ring_pair(p, r)
            begin(at, f)
            begin(at + 2, g)

        for src, dst in (((ua, na), (ub, nb)), ((ub, nb), (uc, nc))):
            def power(i, _):
                at = i * PB + 1
                u, n = neighbours(at, PB, src)
                dst[0][pl.ds(at, PB)] = u * keep
                dst[1][pl.ds(at, PB)] = n * keep_near
                return None

            loop(136 // PB, power)

        def last(i, _):
            at = i * PB + 1
            put = pl.ds(at, PB)
            u, n = neighbours(at, PB, (uc, nc))
            o = full(own, PB)
            u3 = jnp.where(o, u, n)
            u2 = jnp.where(o, uc[put], nc[put])
            u1 = jnp.where(o, ub[put], nb[put])
            u0 = jnp.where(o, ua[put], na[put])
            zx[put] = coef_ref[0] * u0 + coef_ref[1] * u1 + coef_ref[2] * u2 + coef_ref[3] * u3
            return None

        loop(136 // PB, last)

        def image(i, _):
            at = i * B + 5
            o = full(own, B)
            lo = neighbours(at, B, (zx,))[0] * dg[pl.ds(at, B)]
            hi = neighbours(at + 64, B, (zx,))[0] * dg[pl.ds(at + 64, B)]
            sc[pl.ds(i * B, B)] = jnp.where(o, lo, swap(hi))
            zc[pl.ds(i * B, B)] = jnp.where(o, zx[pl.ds(at, B)], swap(zx[pl.ds(at + 64, B)]))
            return None

        loop(64 // B, image)

    hcols = []
    beta = None
    for k in range(M):
        arrive(copies[k])
        red_middle(k)
        precondition_image(k)
        rows = rows_of(red_end(k), k + 1)
        if k == 0:
            beta = jnp.sqrt(rows[0])
            scale = 1.0 / beta
            h = []
        else:
            h = rows[:k]
            square = rows[k]
            for x in h:
                square = square - x * x
            length = jnp.sqrt(square)
            scale = 1.0 / length
            hcols.append(h + [length])

        def update_q(i, _, k=k, h=h, scale=scale):
            fields = []
            for base in (0, 32):
                put = pl.ds(i * B + base, B)
                q = sc[put]
                for j in range(k):
                    q = q - h[j] * qb[j, put]
                q = q * scale
                qb[k, put] = q
                fields.append(q)
            if k < M - 1:
                pack_pair(k + 1, i * B, fields[0], fields[1])
            return None

        loop(32 // B, update_q)
        if k < M - 1:
            pack_strips(k + 1, qb.at[k])
            copies.append(f_copies(k + 1))
            start(copies[k + 1])

        def update_v(i, accs, k=k, h=h, scale=scale):
            accs = list(accs)
            for base in (0, 32):
                put = pl.ds(i * B + base, B)
                v = rc[put] if k == 0 else qb[k - 1, put]
                q = qb[k, put]
                basis = [vb[j, put] for j in range(k)]
                for j in range(k):
                    v = v - h[j] * basis[j]
                v = v * scale
                vb[k, put] = v
                for j, b in enumerate(basis + [v, q]):
                    accs[j] = accs[j] + jnp.sum(q * b, axis=0)
            return tuple(accs)

        accs = loop(32 // B, update_v, tuple(jnp.zeros((8, 128), F32) for _ in range(k + 2)))
        red_start(k + 1, 0, tile_of(accs))

        def update_z(i, _, k=k, h=h, scale=scale):
            for base in (0, 32):
                put = pl.ds(i * B + base, B)
                z = zc[put]
                for j in range(k):
                    z = z - h[j] * zb[j, put]
                zb[k, put] = z * scale
            return None

        loop(32 // B, update_z)

    red_middle(M)
    rows = rows_of(red_end(M), M + 1)
    square = rows[M]
    for x in rows[:M]:
        square = square - x * x
    hcols.append(rows[:M] + [jnp.sqrt(square)])

    g = [beta] + [jnp.zeros((8, 128), F32)] * M
    turns = []
    upper = []
    for k in range(M):
        col = list(hcols[k])
        for j, (c, s) in enumerate(turns):
            col[j], col[j + 1] = c * col[j] + s * col[j + 1], c * col[j + 1] - s * col[j]
        rad = jnp.sqrt(col[k] * col[k] + col[k + 1] * col[k + 1])
        c, s = col[k] / rad, col[k + 1] / rad
        turns.append((c, s))
        col[k] = c * col[k] + s * col[k + 1]
        upper.append(col)
        g[k], g[k + 1] = c * g[k] + s * g[k + 1], c * g[k + 1] - s * g[k]
    y = [None] * M
    for k in reversed(range(M)):
        run = g[k]
        for later in range(k + 1, M):
            run = run - upper[later][k] * y[later]
        y[k] = run / upper[k][k]

    def combine(i, _):
        put = pl.ds(i * B, B)
        z = y[0] * zb[0, put]
        r = rc[put] - y[0] * qb[0, put]
        for k in range(1, M):
            z = z + y[k] * zb[k, put]
            r = r - y[k] * qb[k, put]
        zc[put] = z
        sc[put] = r
        return None

    loop(64 // B, combine)

    def store_packed(src, dst):
        planes = jnp.swapaxes(src[...], 0, 1)
        for x in range(8):
            t = planes[x].T
            dst[x] = jnp.concatenate([t[:64], t[64:]], axis=1)

    store_packed(zc, sol_ref)
    store_packed(sc, res_ref)

    leave(kcop)
    for c in copies:
        leave(c)
    for phase in range(M + 1):
        for stage in range(1 if direct else 2):
            for copy in red_copies(phase, stage, True):
                copy.wait_send()


def local(nsx, nsy, rhs_field, conduct, intersections, poly_coef):
    assert rhs_field.shape == (8, 64, 128)
    vmem = pl.BlockSpec(memory_space=pltpu.VMEM)
    smem = pl.BlockSpec(memory_space=pltpu.SMEM)
    packed = (64, 8, 128)
    ring = (138, 8, 128)
    dma = pltpu.SemaphoreType.DMA
    slots = nsx * nsy if nsx * nsy <= 16 else nsx
    scratch = (
        [pltpu.VMEM(packed, F32)] * 2
        + [pltpu.VMEM((M,) + packed, F32)] * 3
        + [pltpu.VMEM(packed, F32)] * 2
        + [pltpu.VMEM(ring, F32)] * 16
        + [
            pltpu.VMEM((M, 2, 32, 8, 128), F32),
            pltpu.VMEM((M, 2, OV, 8, 128), F32),
            pltpu.VMEM((M, 2, 32, 8, 128), F32),
            pltpu.VMEM((M, 6, 2, 8, 128), F32),
            pltpu.VMEM((2,) + packed, F32),
            pltpu.VMEM((6, OV + 1, 8, 128), F32),
            pltpu.VMEM((M + 1, slots, 8, 128), F32),
            pltpu.VMEM((M + 1, nsy, 8, 128), F32),
            dma((M, 2)), dma((M, 2)), dma((M, 6)), dma((M, 6)),
            dma((2,)), dma((2,)), dma((6,)), dma((6,)),
            dma((M + 1, slots)), dma((M + 1, slots)), dma((M + 1, nsy)), dma((M + 1, nsy)),
        ]
    )
    out = jax.ShapeDtypeStruct(rhs_field.shape, F32)
    return pl.pallas_call(
        functools.partial(kernel, nsx, nsy),
        out_shape=(out, out),
        in_specs=[vmem, vmem, smem, smem],
        out_specs=(vmem, vmem),
        scratch_shapes=scratch,
        compiler_params=pltpu.CompilerParams(
            collective_id=0, has_side_effects=True, vmem_limit_bytes=40 * 1024 * 1024
        ),
        name="gmres_cycle",
    )(rhs_field, conduct, intersections, poly_coef)


def solution(mesh):
    nsx, nsy = mesh.shape["sx"], mesh.shape["sy"]
    spec = P(("grp", "sx"), None, "sy")
    return jax.shard_map(
        functools.partial(local, nsx, nsy),
        mesh=mesh,
        in_specs=(spec, spec, P("grp", None), P()),
        out_specs=(spec, spec),
        check_vma=False,
    )
```
